32 devices in a mesh: seq: 8 (over z, y), blk: 2 (over x), grp: 2 (over core).
Axes of the slice: x: 2, y: 2, z: 4, core: 2. Of those that a mesh axis runs over, the one named last changes fastest.
Arguments:
- activations: bfloat16 [8192, 2048], P('seq', 'blk'), may hold values from -23 to 23
- cotangent: bfloat16 [8192, 1024], P('seq'), may hold values from -0.09375 to 0.09375
- factor: float32 [2048, 1024], P('blk', ('seq', 'grp')), may hold values from -0.3 to 1.7
Outputs:
- new_factor: float32 [2048, 1024], P('blk', ('seq', 'grp'))
- direction: float32 [2048, 1024], P('blk', ('seq', 'grp'))
The draws below stay inside these ranges and needn't reach their ends.
All inputs are finite; a program needn't handle non-finite values.
Results may differ from the reference program's by a relative error of at most 0.007.
Values may be sent and summed in bfloat16 or wider, within the bound.
A program may use at most 64 MiB of HBM per device.

```python
import math
import jax
import jax.numpy as jnp

B = 1024
DOUT = 1024
D = 2048
TOKENS = 8192


def draw_activations(key, part):
    first, second, third = jax.random.split(key, 3)
    values = jnp.clip(jax.random.normal(first, (TOKENS, D), jnp.float32), -4.0, 4.0)
    row_scale = jnp.exp(jax.random.uniform(second, (TOKENS, 1), jnp.float32, math.log(0.2), math.log(2.0)))
    rising = jnp.sqrt(0.5 + 1.5 * jnp.arange(TOKENS, dtype=jnp.float32) / TOKENS)[:, None]
    column_scale = jnp.exp(jax.random.uniform(third, (1, D), jnp.float32, math.log(0.5), math.log(2.0)))
    return (values * row_scale * rising * column_scale).astype(jnp.bfloat16)


def draw_factor(key, part):
    first, second = jax.random.split(key, 2)
    spread = 0.5 / math.sqrt(B)
    off_diag = jnp.clip(jax.random.normal(first, (D, B), jnp.float32), -4.0, 4.0) * spread
    diag_scale = jnp.exp(jax.random.uniform(second, (D, 1), jnp.float32, math.log(0.7), math.log(1.4)))
    on_diag = (jnp.arange(D)[:, None] % B == jnp.arange(B)[None, :]).astype(jnp.float32)
    return off_diag + on_diag * diag_scale


def with_spikes(result, rng, source, target, blocks, factor):
    def block_of(axis_at):
        return (jnp.arange(result.shape[axis_at]) // (result.shape[axis_at] // blocks)).reshape((-1,) + (1,) * (result.ndim - 1 - axis_at))

    first = jax.random.permutation(rng, blocks)[block_of(target)]
    far = (block_of(target) + blocks // 2) % blocks
    return jnp.where((block_of(source) == first) | (block_of(source) == far), factor * result, result)


def steps_of(stream_key, dims, cuts, least, largest):
    factor_of, own = 1.0, jax.random.fold_in(stream_key, 6)
    for axis_at, blocks in cuts:
        heights = jnp.exp(jax.random.uniform(jax.random.fold_in(own, axis_at), (blocks,), jnp.float32, least / len(cuts), largest / len(cuts)))
        factor_of = factor_of * jnp.repeat(heights, dims[axis_at] // blocks).reshape([-1 if axis == axis_at else 1 for axis in range(len(dims))])
    return factor_of


def noise_with(rng, dims, width, limit, cuts, heavy, held_as=jnp.bfloat16):
    array = width * jax.random.normal(rng, dims, jnp.float32)
    if cuts:
        array = array * steps_of(rng, dims, cuts, -0.22, 0.18)
    return jnp.clip(with_spikes(array, jax.random.fold_in(rng, 3), *heavy), -limit, limit).astype(held_as)


def setup_inputs(seed: int = 0) -> dict:
    key_list = jax.random.split(jax.random.key(seed), 4)
    activations = draw_activations(jax.random.fold_in(key_list[3], 71), 0)
    cotangent = noise_with(key_list[1], (TOKENS, DOUT), (TOKENS ** -0.5), 0.09375, ((0, 8),), (0, 1, 8, 2.0))
    factor = draw_factor(jax.random.fold_in(key_list[3], 71), 0)
    return {"activations": activations, "cotangent": cotangent, "factor": factor}


damping = 0.25
step_size = 0.4


def reference(activations, cotangent, factor):
    factor_low = factor.astype(jnp.bfloat16)
    identity = jnp.eye(B, dtype=jnp.float32)
    new_blocks = []
    direction_blocks = []
    for block in range(D // B):
        block_factor = factor_low[block * B:(block + 1) * B]
        inputs = activations[:, block * B:(block + 1) * B]
        whitened = jnp.dot(inputs, block_factor, preferred_element_type=jnp.float32).astype(jnp.bfloat16)
        gram = jnp.dot(whitened.T, whitened, preferred_element_type=jnp.float32)
        cross = jnp.dot(block_factor.T, block_factor, preferred_element_type=jnp.float32)
        curvature = (gram / TOKENS + damping * cross - identity).astype(jnp.bfloat16)
        update = jnp.dot(block_factor, curvature, preferred_element_type=jnp.float32)
        new_blocks.append(factor[block * B:(block + 1) * B] - 0.5 * step_size * update)
        gradient = jnp.dot(inputs.T, cotangent, preferred_element_type=jnp.float32).astype(jnp.bfloat16)
        half = jnp.dot(block_factor.T, gradient, preferred_element_type=jnp.float32).astype(jnp.bfloat16)
        direction_blocks.append(jnp.dot(block_factor, half, preferred_element_type=jnp.float32))
    return jnp.concatenate(new_blocks, axis=0), jnp.concatenate(direction_blocks, axis=0)
```

```python
import functools

import jax
import jax.numpy as jnp
from jax import lax
from jax.experimental import pallas as pl
from jax.experimental.pallas import tpu as pltpu
from jax.sharding import PartitionSpec as P

damping = 0.25
step_size = 0.4

NT = (((1,), (1,)), ((), ()))
NN = (((1,), (0,)), ((), ()))
MESH = pl.DeviceIdType.MESH


def dot(left, right, dims):
    return lax.dot_general(left, right, dims, preferred_element_type=jnp.float32)


def kernel(
    n, grps, total_tokens,
    a_hbm, c_hbm, f_ref, new_ref, dir_ref,
    a, c, ct, kt, wt, send_buf, recv_buf,
    local_sem, ag_send, ag_recv, pair_send, pair_recv, rs_send, rs_recv,
):
    hops = n // 2
    lines = 4 if n % 4 == 0 else 1
    per_line = n // lines
    width, owned = f_ref.shape
    half = width // 2
    me = lax.axis_index("seq")
    grp = lax.axis_index("grp")

    my_y, my_z = lax.rem(me, per_line), lax.div(me, per_line)
    pos = my_y * lines + my_z + lax.rem(my_y, 2) * (lines - 1 - 2 * my_z)

    def at(offset):
        place = lax.rem(pos + offset + n, n)
        y, t = lax.div(place, lines), lax.rem(place, lines)
        return (t + lax.rem(y, 2) * (lines - 1 - 2 * t)) * per_line + y

    neighbour = (at(1), at(-1))
    sign = (1, -1)
    partners = [lax.rem(grp + j, grps) for j in range(1, grps)]

    def rows(offset, g=None):
        g = grp if g is None else g
        return pl.ds(pl.multiple_of((at(offset) * grps + g) * owned, owned), owned)

    def pair_rows(offset):
        return pl.ds(pl.multiple_of(at(offset) * grps * owned, grps * owned), grps * owned)

    def cols(h):
        return pl.ds(h * half, half)

    load_a = pltpu.make_async_copy(a_hbm, a, local_sem.at[0])
    load_c = pltpu.make_async_copy(c_hbm, c, local_sem.at[1])
    load_c.start()
    load_a.start()

    barrier = pltpu.get_barrier_semaphore()
    for d in range(2):
        pl.semaphore_signal(barrier, inc=1, device_id={"seq": neighbour[d]}, device_id_type=MESH)
    for other in partners:
        pl.semaphore_signal(barrier, inc=1, device_id={"grp": other}, device_id_type=MESH)
    kt[rows(0), :] = jnp.transpose(f_ref[...]).astype(jnp.bfloat16)
    pl.semaphore_wait(barrier, 2 + len(partners))

    started = []

    def ag_copy(d, k, h, offset):
        piece = kt.at[rows(offset), cols(h)]
        return pltpu.make_async_remote_copy(
            src_ref=piece, dst_ref=piece,
            send_sem=ag_send.at[d, k - 1, h], recv_sem=ag_recv.at[d, k - 1, h],
            device_id={"seq": neighbour[d]}, device_id_type=MESH,
        )

    def ag_start(d, k, h):
        if k == hops and h != d:
            return
        copy = ag_copy(d, k, h, -sign[d] * (k - 1))
        copy.start()
        started.append(copy)

    def pair_copy(d, k, h, j, offset, g):
        piece = kt.at[rows(offset, g), cols(h)]
        return pltpu.make_async_remote_copy(
            src_ref=piece, dst_ref=piece,
            send_sem=pair_send.at[d, k, h, j], recv_sem=pair_recv.at[d, k, h, j],
            device_id={"grp": partners[j]}, device_id_type=MESH,
        )

    def pair_start(d, k, h):
        for j in range(len(partners)):
            copy = pair_copy(d, k, h, j, -sign[d] * k, grp)
            copy.start()
            started.append(copy)

    def pair_wait(d, k, h):
        for j in range(len(partners)):
            source = lax.rem(grp - (j + 1) + grps, grps)
            pair_copy(d, k, h, j, -sign[d] * k, source).wait_recv()

    def ag_hop(k):
        for h in range(2):
            for d in range(2):
                e = h if d == 0 else 1 - h
                if k == hops and e != d:
                    continue
                ag_copy(d, k, e, -sign[d] * k).wait_recv()
                if k < hops:
                    ag_start(d, k + 1, e)
                pair_start(d, k, e)

    def whiten(k):
        offsets = (0,) if k == 0 else ((hops,) if k == hops else (-k, k))
        for d in range(2):
            for h in range(2):
                if (k == 0 and d == 1) or (k == hops and h != d):
                    continue
                pair_wait(d, k, h)
        lhs = [kt[pair_rows(o), :] for o in offsets]
        lhs = lhs[0] if len(lhs) == 1 else jnp.concatenate(lhs, 0)
        out = dot(lhs, a[...], NT).astype(jnp.bfloat16)
        for i, o in enumerate(offsets):
            wt[pair_rows(o), :] = out[i * grps * owned:(i + 1) * grps * owned]

    def rs_copy(r, d, k, h):
        return pltpu.make_async_remote_copy(
            src_ref=send_buf.at[r, d, k - 1, :, cols(h)], dst_ref=recv_buf.at[r, d, k - 1, :, cols(h)],
            send_sem=rs_send.at[r, d, k - 1, h], recv_sem=rs_recv.at[r, d, k - 1, h],
            device_id={"seq": neighbour[d]}, device_id_type=MESH,
        )

    def rs_hop(r, k, partial):
        far = hops + 1 - k
        if k == 1:
            own = partial((far,))[0]
        else:
            own = partial((far, -far))
        for h in range(2):
            for d in range(2):
                e = h if d == 0 else 1 - h
                if k == 1:
                    if e != d:
                        continue
                    value = own[:, e * half:(e + 1) * half]
                else:
                    value = own[d][:, e * half:(e + 1) * half]
                    if k > 2 or e == d:
                        rs_copy(r, d, k - 1, e).wait_recv()
                        value = value + recv_buf[r, d, k - 2, :, cols(e)].astype(jnp.float32)
                send_buf[r, d, k - 1, :, cols(e)] = value.astype(jnp.bfloat16)
                copy = rs_copy(r, d, k, e)
                copy.start()
                started.append(copy)

    def rs_last(r, own):
        parts = []
        for e in range(2):
            value = own[:, e * half:(e + 1) * half]
            for d in range(2):
                rs_copy(r, d, hops, e).wait_recv()
                value = value + recv_buf[r, d, hops - 1, :, cols(e)].astype(jnp.float32)
            parts.append(value)
        return jnp.concatenate(parts, 1)

    def rows_of(ref, offsets):
        taken = [ref[rows(o), :] for o in offsets]
        return taken[0] if len(taken) == 1 else jnp.concatenate(taken, 0)

    def split(value, offsets):
        return [value[i * owned:(i + 1) * owned] for i in range(len(offsets))]

    def grad_part(offsets):
        return split(dot(rows_of(ct, offsets), a[...], NN), offsets)

    def gram_part(offsets):
        return split(dot(rows_of(wt, offsets), wt[...], NT), offsets)

    for h in range(2):
        for d in range(2):
            ag_start(d, 1, h if d == 0 else 1 - h)
    for h in range(2):
        pair_start(0, 0, h)

    load_c.wait()
    ct[...] = jnp.transpose(c[...])
    load_a.wait()
    rs_hop(0, 1, grad_part)
    whiten(0)
    early = hops // 2
    for k in range(1, hops + 1):
        ag_hop(k)
        if 2 <= k + 1 <= early:
            rs_hop(0, k + 1, grad_part)
        if k < hops:
            whiten(k)
    whiten(hops)
    rs_hop(1, 1, gram_part)
    cross = dot(kt[rows(0), :], kt[...], NT)
    for k in range(early + 1, hops + 1):
        rs_hop(0, k, grad_part)
        if 2 <= k - early + 1 <= hops:
            rs_hop(1, k - early + 1, gram_part)
    for k in range(hops - early + 2, hops + 1):
        rs_hop(1, k, gram_part)
    gradient = rs_last(0, grad_part((0,))[0]).astype(jnp.bfloat16)
    halved = dot(gradient, kt[...], NT).astype(jnp.bfloat16)
    dir_ref[...] = jnp.transpose(dot(halved, kt[...], NN))
    first = (me * grps + grp) * owned
    line = lax.broadcasted_iota(jnp.int32, (owned, width), 0) + first
    identity = (line == lax.broadcasted_iota(jnp.int32, (owned, width), 1)).astype(jnp.float32)
    own_gram = gram_part((0,))[0]
    gram = rs_last(1, own_gram)
    curvature = (gram / total_tokens + damping * cross - identity).astype(jnp.bfloat16)
    update = dot(curvature, kt[...], NN)
    new_ref[...] = f_ref[...] - 0.5 * step_size * jnp.transpose(update)
    for copy in started:
        copy.wait_send()


def on_device(n, grps, activations, cotangent, factor):
    tokens, width = activations.shape
    out_width = cotangent.shape[1]
    owned = factor.shape[1]
    hops = n // 2
    low = jnp.bfloat16
    pairs = max(grps - 1, 1)
    dma = pltpu.SemaphoreType.DMA
    vmem = pl.BlockSpec(memory_space=pltpu.VMEM)
    flops = 2 * tokens * width * (width + width // grps + out_width // grps)
    return pl.pallas_call(
        functools.partial(kernel, n, grps, tokens * n),
        out_shape=(
            jax.ShapeDtypeStruct((width, owned), jnp.float32),
            jax.ShapeDtypeStruct((width, owned), jnp.float32),
        ),
        in_specs=[pl.BlockSpec(memory_space=pl.ANY)] * 2 + [vmem],
        out_specs=(vmem, vmem),
        scratch_shapes=[
            pltpu.VMEM((tokens, width), low),
            pltpu.VMEM((tokens, out_width), low),
            pltpu.VMEM((out_width, tokens), low),
            pltpu.VMEM((width, width), low),
            pltpu.VMEM((width, tokens), low),
            pltpu.VMEM((2, 2, hops, owned, width), low),
            pltpu.VMEM((2, 2, hops, owned, width), low),
            dma((2,)),
            dma((2, hops, 2)),
            dma((2, hops, 2)),
            dma((2, hops + 1, 2, pairs)),
            dma((2, hops + 1, 2, pairs)),
            dma((2, 2, hops, 2)),
            dma((2, 2, hops, 2)),
        ],
        compiler_params=pltpu.CompilerParams(
            collective_id=0, has_side_effects=True, vmem_limit_bytes=48 * 1024 * 1024
        ),
        cost_estimate=pl.CostEstimate(
            flops=flops, bytes_accessed=4 * tokens * width, transcendentals=0
        ),
    )(activations, cotangent, factor)


def solution(mesh):
    placed = (P("seq", "blk"), P("seq", None), P("blk", ("seq", "grp")))
    return jax.shard_map(
        functools.partial(on_device, mesh.shape["seq"], mesh.shape["grp"]),
        mesh=mesh,
        in_specs=placed,
        out_specs=(P("blk", ("seq", "grp")), P("blk", ("seq", "grp"))),
        check_vma=False,
    )
```

```python
import functools

import jax
import jax.numpy as jnp
from jax import lax
from jax.experimental import pallas as pl
from jax.experimental.pallas import tpu as pltpu
from jax.sharding import PartitionSpec as P

damping = 0.25
step_size = 0.4

NT = (((1,), (1,)), ((), ()))
NN = (((1,), (0,)), ((), ()))
MESH = pl.DeviceIdType.MESH


def dot(left, right, dims):
    return lax.dot_general(left, right, dims, preferred_element_type=jnp.float32)


def kernel(
    n, grps, total_tokens,
    a_hbm, c_hbm, f_ref, new_ref, dir_ref,
    a, c, ct, kt, wt, send_buf, recv_buf,
    local_sem, ag_send, ag_recv, pair_send, pair_recv, rs_send, rs_recv,
):
    hops = n // 2
    lines = 4 if n % 4 == 0 else 1
    per_line = n // lines
    owned, width = f_ref.shape
    half = width // 2
    me = lax.axis_index("seq")
    grp = lax.axis_index("grp")

    my_y, my_z = lax.rem(me, per_line), lax.div(me, per_line)
    pos = my_y * lines + my_z + lax.rem(my_y, 2) * (lines - 1 - 2 * my_z)

    def at(offset):
        place = lax.rem(pos + offset + n, n)
        y, t = lax.div(place, lines), lax.rem(place, lines)
        return (t + lax.rem(y, 2) * (lines - 1 - 2 * t)) * per_line + y

    neighbour = (at(1), at(-1))
    sign = (1, -1)
    partners = [lax.rem(grp + j, grps) for j in range(1, grps)]

    def rows(offset, g=None):
        g = grp if g is None else g
        return pl.ds(pl.multiple_of((at(offset) * grps + g) * owned, owned), owned)

    def pair_rows(offset):
        return pl.ds(pl.multiple_of(at(offset) * grps * owned, grps * owned), grps * owned)

    def cols(h):
        return pl.ds(h * half, half)

    load_a = pltpu.make_async_copy(a_hbm, a, local_sem.at[0])
    load_c = pltpu.make_async_copy(c_hbm, c, local_sem.at[1])
    load_c.start()
    load_a.start()

    barrier = pltpu.get_barrier_semaphore()
    for d in range(2):
        pl.semaphore_signal(barrier, inc=1, device_id={"seq": neighbour[d]}, device_id_type=MESH)
    for other in partners:
        pl.semaphore_signal(barrier, inc=1, device_id={"grp": other}, device_id_type=MESH)
    kt[rows(0), :] = f_ref[...].astype(jnp.bfloat16)
    pl.semaphore_wait(barrier, 2 + len(partners))

    started = []

    def ag_copy(d, k, h, offset):
        piece = kt.at[rows(offset), cols(h)]
        return pltpu.make_async_remote_copy(
            src_ref=piece, dst_ref=piece,
            send_sem=ag_send.at[d, k - 1, h], recv_sem=ag_recv.at[d, k - 1, h],
            device_id={"seq": neighbour[d]}, device_id_type=MESH,
        )

    def ag_start(d, k, h):
        if k == hops and h != d:
            return
        copy = ag_copy(d, k, h, -sign[d] * (k - 1))
        copy.start()
        started.append(copy)

    def pair_copy(d, k, h, j, offset, g):
        piece = kt.at[rows(offset, g), cols(h)]
        return pltpu.make_async_remote_copy(
            src_ref=piece, dst_ref=piece,
            send_sem=pair_send.at[d, k, h, j], recv_sem=pair_recv.at[d, k, h, j],
            device_id={"grp": partners[j]}, device_id_type=MESH,
        )

    def pair_start(d, k, h):
        for j in range(len(partners)):
            copy = pair_copy(d, k, h, j, -sign[d] * k, grp)
            copy.start()
            started.append(copy)

    def pair_wait(d, k, h):
        for j in range(len(partners)):
            source = lax.rem(grp - (j + 1) + grps, grps)
            pair_copy(d, k, h, j, -sign[d] * k, source).wait_recv()

    def ag_hop(k):
        for h in range(2):
            for d in range(2):
                e = h if d == 0 else 1 - h
                if k == hops and e != d:
                    continue
                ag_copy(d, k, e, -sign[d] * k).wait_recv()
                if k < hops:
                    ag_start(d, k + 1, e)
                pair_start(d, k, e)

    def whiten(k):
        offsets = (0,) if k == 0 else ((hops,) if k == hops else (-k, k))
        for d in range(2):
            for h in range(2):
                if (k == 0 and d == 1) or (k == hops and h != d):
                    continue
                pair_wait(d, k, h)
        lhs = [kt[pair_rows(o), :] for o in offsets]
        lhs = lhs[0] if len(lhs) == 1 else jnp.concatenate(lhs, 0)
        out = dot(lhs, a[...], NT).astype(jnp.bfloat16)
        for i, o in enumerate(offsets):
            wt[pair_rows(o), :] = out[i * grps * owned:(i + 1) * grps * owned]

    def rs_copy(r, d, k, h):
        return pltpu.make_async_remote_copy(
            src_ref=send_buf.at[r, d, k - 1, h], dst_ref=recv_buf.at[r, d, k - 1, h],
            send_sem=rs_send.at[r, d, k - 1, h], recv_sem=rs_recv.at[r, d, k - 1, h],
            device_id={"seq": neighbour[d]}, device_id_type=MESH,
        )

    def rs_hop(r, k, partial):
        far = hops + 1 - k
        if k == 1:
            own = partial((far,))[0]
        else:
            own = partial((far, -far))
        for h in range(2):
            for d in range(2):
                e = h if d == 0 else 1 - h
                if k == 1:
                    if e != d:
                        continue
                    value = own[:, e * half:(e + 1) * half]
                else:
                    value = own[d][:, e * half:(e + 1) * half]
                    if k > 2 or e == d:
                        rs_copy(r, d, k - 1, e).wait_recv()
                        value = value + recv_buf[r, d, k - 2, e].astype(jnp.float32)
                send_buf[r, d, k - 1, e] = value.astype(jnp.bfloat16)
                copy = rs_copy(r, d, k, e)
                copy.start()
                started.append(copy)

    def rs_last(r, own):
        parts = []
        for e in range(2):
            value = own[:, e * half:(e + 1) * half]
            for d in range(2):
                rs_copy(r, d, hops, e).wait_recv()
                value = value + recv_buf[r, d, hops - 1, e].astype(jnp.float32)
            parts.append(value)
        return jnp.concatenate(parts, 1)

    def rows_of(ref, offsets):
        taken = [ref[rows(o), :] for o in offsets]
        return taken[0] if len(taken) == 1 else jnp.concatenate(taken, 0)

    def split(value, offsets):
        return [value[i * owned:(i + 1) * owned] for i in range(len(offsets))]

    def grad_part(offsets):
        return split(dot(rows_of(ct, offsets), a[...], NN), offsets)

    def gram_part(offsets):
        return split(dot(rows_of(wt, offsets), wt[...], NT), offsets)

    for h in range(2):
        for d in range(2):
            ag_start(d, 1, h if d == 0 else 1 - h)
    for h in range(2):
        pair_start(0, 0, h)

    load_c.wait()
    ct[...] = jnp.transpose(c[...])
    load_a.wait()
    rs_hop(0, 1, grad_part)
    whiten(0)
    early = hops
    for k in range(1, hops + 1):
        ag_hop(k)
        if 2 <= k + 1 <= early:
            rs_hop(0, k + 1, grad_part)
        if k < hops:
            whiten(k)
    whiten(hops)
    rs_hop(1, 1, gram_part)
    cross = dot(kt[rows(0), :], kt[...], NT)
    for k in range(early + 1, hops + 1):
        rs_hop(0, k, grad_part)
        if 2 <= k - early + 1 <= hops:
            rs_hop(1, k - early + 1, gram_part)
    for k in range(hops - early + 2, hops + 1):
        rs_hop(1, k, gram_part)
    gradient = rs_last(0, grad_part((0,))[0]).astype(jnp.bfloat16)
    halved = dot(gradient, kt[...], NT).astype(jnp.bfloat16)
    dir_ref[...] = dot(halved, kt[...], NN)
    first = (me * grps + grp) * owned
    line = lax.broadcasted_iota(jnp.int32, (owned, width), 0) + first
    identity = (line == lax.broadcasted_iota(jnp.int32, (owned, width), 1)).astype(jnp.float32)
    own_gram = gram_part((0,))[0]
    gram = rs_last(1, own_gram)
    curvature = (gram / total_tokens + damping * cross - identity).astype(jnp.bfloat16)
    update = dot(curvature, kt[...], NN)
    new_ref[...] = f_ref[...] - 0.5 * step_size * update
    for copy in started:
        copy.wait_send()


def on_device(n, grps, activations, cotangent, factor):
    tokens, width = activations.shape
    out_width = cotangent.shape[1]
    owned = factor.shape[1]
    hops = n // 2
    low = jnp.bfloat16
    pairs = max(grps - 1, 1)
    dma = pltpu.SemaphoreType.DMA
    vmem = pl.BlockSpec(memory_space=pltpu.VMEM)
    flops = 2 * tokens * width * (width + width // grps + out_width // grps)
    new_rows, direction_rows = pl.pallas_call(
        functools.partial(kernel, n, grps, tokens * n),
        out_shape=(
            jax.ShapeDtypeStruct((owned, width), jnp.float32),
            jax.ShapeDtypeStruct((owned, width), jnp.float32),
        ),
        in_specs=[pl.BlockSpec(memory_space=pl.ANY)] * 2 + [vmem],
        out_specs=(vmem, vmem),
        scratch_shapes=[
            pltpu.VMEM((tokens, width), low),
            pltpu.VMEM((tokens, out_width), low),
            pltpu.VMEM((out_width, tokens), low),
            pltpu.VMEM((width, width), low),
            pltpu.VMEM((width, tokens), low),
            pltpu.VMEM((2, 2, hops, 2, owned, width // 2), low),
            pltpu.VMEM((2, 2, hops, 2, owned, width // 2), low),
            dma((2,)),
            dma((2, hops, 2)),
            dma((2, hops, 2)),
            dma((2, hops + 1, 2, pairs)),
            dma((2, hops + 1, 2, pairs)),
            dma((2, 2, hops, 2)),
            dma((2, 2, hops, 2)),
        ],
        compiler_params=pltpu.CompilerParams(
            collective_id=0, has_side_effects=True, vmem_limit_bytes=62 * 1024 * 1024
        ),
        cost_estimate=pl.CostEstimate(
            flops=flops, bytes_accessed=4 * tokens * width, transcendentals=0
        ),
    )(activations, cotangent, factor.T)
    return new_rows.T, direction_rows.T


def solution(mesh):
    placed = (P("seq", "blk"), P("seq", None), P("blk", ("seq", "grp")))
    return jax.shard_map(
        functools.partial(on_device, mesh.shape["seq"], mesh.shape["grp"]),
        mesh=mesh,
        in_specs=placed,
        out_specs=(P("blk", ("seq", "grp")), P("blk", ("seq", "grp"))),
        check_vma=False,
    )
```

```python
import functools

import jax
import jax.numpy as jnp
from jax import lax
from jax.experimental import pallas as pl
from jax.experimental.pallas import tpu as pltpu
from jax.sharding import PartitionSpec as P

damping = 0.25
step_size = 0.4

NT = (((1,), (1,)), ((), ()))
NN = (((1,), (0,)), ((), ()))
MESH = pl.DeviceIdType.MESH


def dot(left, right, dims):
    return lax.dot_general(left, right, dims, preferred_element_type=jnp.float32)


def kernel(
    n, grps, total_tokens,
    a_hbm, c_hbm, f_ref, new_ref, dir_ref,
    a, c, ct, kt, wt, send_buf, recv_buf,
    local_sem, ag_send, ag_recv, pair_send, pair_recv, rs_send, rs_recv,
):
    hops = n // 2
    lines = 4 if n % 4 == 0 else 1
    per_line = n // lines
    owned, width = f_ref.shape
    half = width // 2
    me = lax.axis_index("seq")
    grp = lax.axis_index("grp")

    my_y, my_z = lax.rem(me, per_line), lax.div(me, per_line)
    pos = my_y * lines + my_z + lax.rem(my_y, 2) * (lines - 1 - 2 * my_z)

    def at(offset):
        place = lax.rem(pos + offset + n, n)
        y, t = lax.div(place, lines), lax.rem(place, lines)
        return (t + lax.rem(y, 2) * (lines - 1 - 2 * t)) * per_line + y

    neighbour = (at(1), at(-1))
    sign = (1, -1)
    partners = [lax.rem(grp + j, grps) for j in range(1, grps)]

    def rows(offset, g=None):
        g = grp if g is None else g
        return pl.ds(pl.multiple_of((at(offset) * grps + g) * owned, owned), owned)

    def pair_rows(offset):
        return pl.ds(pl.multiple_of(at(offset) * grps * owned, grps * owned), grps * owned)

    def cols(h):
        return pl.ds(h * half, half)

    load_a = pltpu.make_async_copy(a_hbm, a, local_sem.at[0])
    load_c = pltpu.make_async_copy(c_hbm, c, local_sem.at[1])
    load_c.start()
    load_a.start()

    barrier = pltpu.get_barrier_semaphore()
    for d in range(2):
        pl.semaphore_signal(barrier, inc=1, device_id={"seq": neighbour[d]}, device_id_type=MESH)
    for other in partners:
        pl.semaphore_signal(barrier, inc=1, device_id={"grp": other}, device_id_type=MESH)
    kt[rows(0), :] = f_ref[...].astype(jnp.bfloat16)
    pl.semaphore_wait(barrier, 2 + len(partners))

    started = []

    def ag_copy(d, k, h, offset):
        piece = kt.at[rows(offset), cols(h)]
        return pltpu.make_async_remote_copy(
            src_ref=piece, dst_ref=piece,
            send_sem=ag_send.at[d, k - 1, h], recv_sem=ag_recv.at[d, k - 1, h],
            device_id={"seq": neighbour[d]}, device_id_type=MESH,
        )

    def ag_start(d, k, h):
        if k == hops and h != d:
            return
        copy = ag_copy(d, k, h, -sign[d] * (k - 1))
        copy.start()
        started.append(copy)

    def pair_copy(d, k, h, j, offset, g):
        piece = kt.at[rows(offset, g), cols(h)]
        return pltpu.make_async_remote_copy(
            src_ref=piece, dst_ref=piece,
            send_sem=pair_send.at[d, k, h, j], recv_sem=pair_recv.at[d, k, h, j],
            device_id={"grp": partners[j]}, device_id_type=MESH,
        )

    def pair_start(d, k, h):
        for j in range(len(partners)):
            copy = pair_copy(d, k, h, j, -sign[d] * k, grp)
            copy.start()
            started.append(copy)

    def pair_wait(d, k, h):
        for j in range(len(partners)):
            source = lax.rem(grp - (j + 1) + grps, grps)
            pair_copy(d, k, h, j, -sign[d] * k, source).wait_recv()

    def ag_hop(k):
        for h in range(2):
            for d in range(2):
                e = h if d == 0 else 1 - h
                if k == hops and e != d:
                    continue
                ag_copy(d, k, e, -sign[d] * k).wait_recv()
                if k < hops:
                    ag_start(d, k + 1, e)
                pair_start(d, k, e)

    def whiten(k):
        offsets = (0,) if k == 0 else ((hops,) if k == hops else (-k, k))
        for d in range(2):
            for h in range(2):
                if (k == 0 and d == 1) or (k == hops and h != d):
                    continue
                pair_wait(d, k, h)
        lhs = [kt[pair_rows(o), :] for o in offsets]
        lhs = lhs[0] if len(lhs) == 1 else jnp.concatenate(lhs, 0)
        out = dot(lhs, a[...], NT).astype(jnp.bfloat16)
        for i, o in enumerate(offsets):
            wt[pair_rows(o), :] = out[i * grps * owned:(i + 1) * grps * owned]

    def rs_copy(r, d, k, h):
        return pltpu.make_async_remote_copy(
            src_ref=send_buf.at[r, d, k - 1, h], dst_ref=recv_buf.at[r, d, k - 1, h],
            send_sem=rs_send.at[r, d, k - 1, h], recv_sem=rs_recv.at[r, d, k - 1, h],
            device_id={"seq": neighbour[d]}, device_id_type=MESH,
        )

    def rs_hop(r, k, partial):
        far = hops + 1 - k
        if k == 1:
            own = partial((far,))[0]
        else:
            own = partial((far, -far))
        for h in range(2):
            for d in range(2):
                e = h if d == 0 else 1 - h
                if k == 1:
                    if e != d:
                        continue
                    value = own[:, e * half:(e + 1) * half]
                else:
                    value = own[d][:, e * half:(e + 1) * half]
                    if k > 2 or e == d:
                        rs_copy(r, d, k - 1, e).wait_recv()
                        value = value + recv_buf[r, d, k - 2, e].astype(jnp.float32)
                send_buf[r, d, k - 1, e] = value.astype(jnp.bfloat16)
                copy = rs_copy(r, d, k, e)
                copy.start()
                started.append(copy)

    def rs_last(r, own):
        parts = []
        for e in range(2):
            value = own[:, e * half:(e + 1) * half]
            for d in range(2):
                rs_copy(r, d, hops, e).wait_recv()
                value = value + recv_buf[r, d, hops - 1, e].astype(jnp.float32)
            parts.append(value)
        return jnp.concatenate(parts, 1)

    def rows_of(ref, offsets):
        taken = [ref[rows(o), :] for o in offsets]
        return taken[0] if len(taken) == 1 else jnp.concatenate(taken, 0)

    def split(value, offsets):
        return [value[i * owned:(i + 1) * owned] for i in range(len(offsets))]

    def grad_part(offsets):
        return split(dot(rows_of(ct, offsets), a[...], NN), offsets)

    def gram_part(offsets):
        return split(dot(rows_of(wt, offsets), wt[...], NT), offsets)

    for h in range(2):
        for d in range(2):
            ag_start(d, 1, h if d == 0 else 1 - h)
    for h in range(2):
        pair_start(0, 0, h)

    load_c.wait()
    ct[...] = jnp.transpose(c[...])
    load_a.wait()
    early = hops - 1
    for k in range(1, hops + 1):
        ag_hop(k)
        if k <= early:
            rs_hop(0, k, grad_part)
        if k == 1:
            whiten(0)
        if k < hops:
            whiten(k)
    whiten(hops)
    rs_hop(1, 1, gram_part)
    cross = dot(kt[rows(0), :], kt[...], NT)
    for k in range(early + 1, hops + 1):
        rs_hop(0, k, grad_part)
        if 2 <= k - early + 1 <= hops:
            rs_hop(1, k - early + 1, gram_part)
    for k in range(hops - early + 2, hops + 1):
        rs_hop(1, k, gram_part)
    gradient = rs_last(0, grad_part((0,))[0]).astype(jnp.bfloat16)
    halved = dot(gradient, kt[...], NT).astype(jnp.bfloat16)
    dir_ref[...] = dot(halved, kt[...], NN)
    first = (me * grps + grp) * owned
    line = lax.broadcasted_iota(jnp.int32, (owned, width), 0) + first
    identity = (line == lax.broadcasted_iota(jnp.int32, (owned, width), 1)).astype(jnp.float32)
    own_gram = gram_part((0,))[0]
    gram = rs_last(1, own_gram)
    curvature = (gram / total_tokens + damping * cross - identity).astype(jnp.bfloat16)
    update = dot(curvature, kt[...], NN)
    new_ref[...] = f_ref[...] - 0.5 * step_size * update
    for copy in started:
        copy.wait_send()


def on_device(n, grps, activations, cotangent, factor):
    tokens, width = activations.shape
    out_width = cotangent.shape[1]
    owned = factor.shape[1]
    hops = n // 2
    low = jnp.bfloat16
    pairs = max(grps - 1, 1)
    dma = pltpu.SemaphoreType.DMA
    vmem = pl.BlockSpec(memory_space=pltpu.VMEM)
    flops = 2 * tokens * width * (width + width // grps + out_width // grps)
    new_rows, direction_rows = pl.pallas_call(
        functools.partial(kernel, n, grps, tokens * n),
        out_shape=(
            jax.ShapeDtypeStruct((owned, width), jnp.float32),
            jax.ShapeDtypeStruct((owned, width), jnp.float32),
        ),
        in_specs=[pl.BlockSpec(memory_space=pl.ANY)] * 2 + [vmem],
        out_specs=(vmem, vmem),
        scratch_shapes=[
            pltpu.VMEM((tokens, width), low),
            pltpu.VMEM((tokens, out_width), low),
            pltpu.VMEM((out_width, tokens), low),
            pltpu.VMEM((width, width), low),
            pltpu.VMEM((width, tokens), low),
            pltpu.VMEM((2, 2, hops, 2, owned, width // 2), low),
            pltpu.VMEM((2, 2, hops, 2, owned, width // 2), low),
            dma((2,)),
            dma((2, hops, 2)),
            dma((2, hops, 2)),
            dma((2, hops + 1, 2, pairs)),
            dma((2, hops + 1, 2, pairs)),
            dma((2, 2, hops, 2)),
            dma((2, 2, hops, 2)),
        ],
        compiler_params=pltpu.CompilerParams(
            collective_id=0, has_side_effects=True, vmem_limit_bytes=62 * 1024 * 1024
        ),
        cost_estimate=pl.CostEstimate(
            flops=flops, bytes_accessed=4 * tokens * width, transcendentals=0
        ),
    )(activations, cotangent, factor.T)
    return new_rows.T, direction_rows.T


def solution(mesh):
    placed = (P("seq", "blk"), P("seq", None), P("blk", ("seq", "grp")))
    return jax.shard_map(
        functools.partial(on_device, mesh.shape["seq"], mesh.shape["grp"]),
        mesh=mesh,
        in_specs=placed,
        out_specs=(P("blk", ("seq", "grp")), P("blk", ("seq", "grp"))),
        check_vma=False,
    )
```
